256 devices in a mesh: grp: 8 (over z), dom: 32 (over x, y, core).
Axes of the slice: x: 4, y: 4, z: 8, core: 2. Of those that a mesh axis runs over, the one named last changes fastest.
Arguments:
- features: bfloat16 [262144, 512], P(('grp', 'dom')), parts along dimension 0, may hold values from -6 to 6
- send_rows: int32 [512, 128], P(('grp', 'dom')), parts along dimension 0, may hold values from 0 to 1023, as said below
- neighbors: int32 [262144, 4], P(('grp', 'dom')), parts along dimension 0, may hold values from 0 to 1279, as said below
- membership: int32 [262144], P(('grp', 'dom')), parts along dimension 0, may hold values from 0 to 2047, as said below
- coarse_links: int32 [16384, 8], P(('grp', 'dom')), parts along dimension 0, may hold values from 0 to 2047, as said below
- edge_first: bfloat16 [1024, 512], replicated, may hold values from -0.1875 to 0.1875
- edge_second: bfloat16 [512, 512], replicated, may hold values from -0.25 to 0.25
- node_first: bfloat16 [1024, 512], replicated, may hold values from -0.1875 to 0.1875
- node_second: bfloat16 [512, 512], replicated, may hold values from -0.25 to 0.25
- coarse_edge_first: bfloat16 [1024, 512], replicated, may hold values from -0.1875 to 0.1875
- coarse_edge_second: bfloat16 [512, 512], replicated, may hold values from -0.25 to 0.25
- coarse_node_first: bfloat16 [1024, 512], replicated, may hold values from -0.1875 to 0.1875
- coarse_node_second: bfloat16 [512, 512], replicated, may hold values from -0.25 to 0.25
Outputs:
- output_cells: bfloat16 [262144, 512], P(('grp', 'dom')), parts along dimension 0
The draws below stay inside these ranges and needn't reach their ends.
There are 8 independent parts, one for each index of `grp`. The reference program is written for one: setup_inputs(seed, part) draws one part's arguments, and reference() takes and returns one part's arrays. A program takes and returns all parts, laid end to end along the dimension named above; an argument that names none is the same for every part. Nothing has to cross between parts.
Inputs may be any that keep to these rules, and one draw needn't show every extreme that they name: `send_rows`: each row holds 128 distinct local row numbers; row 2d lists what block d sends to block d+1, row 2d+1 what it sends to block d-1. `neighbors`: values below 1024 name a row of the cell's own block; 1024 + j names slot j of the rows from the block below, 1152 + j slot j of the rows from the block above; the first and last blocks never name the missing side. `membership`: cluster c is owned by block c // 64, which lies at most 2 blocks from the cell's block; every cluster has at least one member. `coarse_links`: every source cluster is owned by a block at most 2 blocks from the owner of the target cluster.
All inputs are finite; a program needn't handle non-finite values.
Results may differ from the reference program's by a relative error of at most 0.011.
Values may be sent and summed in bfloat16 or wider, within the bound.
No kernel may reach another device: no remote copies, remote signals or barrier semaphores. Data moves between devices by JAX's collectives and lax.ppermute only.
A program may use at most 128 MiB of HBM per device.

```python
import jax
import jax.numpy as jnp
from jax import lax

H = 512
N_DEV = 1024
HALO = 128
DEG = 4
CDEG = 8
REACH = 2
C_DEV = 64
NODES = 32768
CLUSTERS = 2048
N_DOM = 32


def draw_send_rows(key, part):
    key = jax.random.fold_in(key, 11)
    domains = NODES // N_DEV
    keys = jax.random.split(key, 2 * domains)
    chosen = jax.vmap(lambda single: jax.random.permutation(single, N_DEV)[:HALO])(keys)
    return chosen.astype(jnp.int32)


def draw_neighbors(key, part):
    key = jax.random.fold_in(key, 12)
    domains = NODES // N_DEV
    key_local, key_slot, key_choose = jax.random.split(key, 3)
    local_id = jax.random.randint(key_local, (NODES, DEG), 0, N_DEV)
    slot_id = jax.random.randint(key_slot, (NODES, DEG), 0, 2 * HALO)
    chooser = jax.random.randint(key_choose, (NODES, DEG), 0, 4)
    device = (jnp.arange(NODES) // N_DEV)[:, None]
    row_index = (jnp.arange(NODES) % N_DEV)[:, None]
    column = jnp.arange(DEG)[None, :]
    forced = (row_index < 2 * HALO) & (column == DEG - 1)
    slot_id = jnp.where(forced, row_index, slot_id)
    use_halo = (chooser == 0) | forced
    slot_id = jnp.where((device == 0) & (slot_id < HALO), slot_id + HALO, slot_id)
    slot_id = jnp.where((device == domains - 1) & (slot_id >= HALO), slot_id - HALO, slot_id)
    return jnp.where(use_halo, N_DEV + slot_id, local_id).astype(jnp.int32)


def draw_membership(key, part):
    key = jax.random.fold_in(key, 13)
    domains = NODES // N_DEV
    key_near, key_offset, key_first, key_second = jax.random.split(key, 4)
    device = jnp.arange(NODES) // N_DEV
    row_index = jnp.arange(NODES) % N_DEV
    nearness = jax.random.randint(key_near, (NODES,), 0, 5)
    offset = jax.random.randint(key_offset, (NODES,), -REACH, REACH + 1)
    offset = jnp.where(nearness < 3, 0, offset)
    offset = jnp.where(row_index == C_DEV, REACH, offset)
    owner_dev = jnp.clip(device + offset, 0, domains - 1)
    first_pick = jax.random.randint(key_first, (NODES,), 0, C_DEV)
    second_pick = jax.random.randint(key_second, (NODES,), 0, C_DEV)
    local_id = jnp.minimum(first_pick, second_pick)
    local_id = jnp.where(row_index < C_DEV, row_index, local_id)
    owner_dev = jnp.where(row_index < C_DEV, device, owner_dev)
    return (owner_dev * C_DEV + local_id).astype(jnp.int32)


def draw_coarse_links(key, part):
    key = jax.random.fold_in(key, 14)
    domains = NODES // N_DEV
    key_offset, key_local = jax.random.split(key, 2)
    device = (jnp.arange(CLUSTERS) // C_DEV)[:, None]
    column = jnp.arange(CDEG)[None, :]
    offset = jax.random.randint(key_offset, (CLUSTERS, CDEG), -REACH, REACH + 1)
    offset = jnp.where(column == 0, REACH, offset)
    owner_dev = jnp.clip(device + offset, 0, domains - 1)
    local_id = jax.random.randint(key_local, (CLUSTERS, CDEG), 0, C_DEV)
    return (owner_dev * C_DEV + local_id).astype(jnp.int32)


def block_levels(stream_key, extent, pieces, low, largest):
    def one(dim, shards_of):
        steps = jax.random.uniform(jax.random.fold_in(jax.random.fold_in(stream_key, 6), dim), (shards_of,), jnp.float32, low / len(pieces), largest / len(pieces))
        return jnp.repeat(jnp.exp(steps), extent[dim] // shards_of).reshape((-1,) + (1,) * (len(extent) - dim - 1))

    loudness = one(*pieces[0])
    for cut in pieces[1:]:
        loudness = loudness * one(*cut)
    return loudness


def noise(key, extent, deviation, most, pieces=(), kind=jnp.bfloat16):
    loudness = block_levels(key, extent, pieces, -0.22, 0.18) if pieces else 1.0
    entries = jax.random.normal(key, extent, jnp.float32) * deviation * loudness
    return jnp.minimum(jnp.maximum(entries, -most), most).astype(kind)


def setup_inputs(seed: int = 0, part: int = 0) -> dict:
    streams_of = jax.random.split(jax.random.key(seed), 14)
    part_keys = jax.random.split(jax.random.fold_in(streams_of[13], part), 14)
    return {
        "features": noise(part_keys[0], (NODES, H), 1.0, 6.0, ((0, 32),)),
        "send_rows": draw_send_rows(jax.random.fold_in(jax.random.fold_in(streams_of[13], part), 71), part),
        "neighbors": draw_neighbors(jax.random.fold_in(jax.random.fold_in(streams_of[13], part), 71), part),
        "membership": draw_membership(jax.random.fold_in(jax.random.fold_in(streams_of[13], part), 71), part),
        "coarse_links": draw_coarse_links(jax.random.fold_in(jax.random.fold_in(streams_of[13], part), 71), part),
        "edge_first": noise(streams_of[5], (2 * H, H), (2 * H) ** -0.5, 0.1875),
        "edge_second": noise(streams_of[6], (H, H), H ** -0.5, 0.25),
        "node_first": noise(streams_of[7], (2 * H, H), (2 * H) ** -0.5, 0.1875),
        "node_second": noise(streams_of[8], (H, H), H ** -0.5, 0.25),
        "coarse_edge_first": noise(streams_of[9], (2 * H, H), (2 * H) ** -0.5, 0.1875),
        "coarse_edge_second": noise(streams_of[10], (H, H), H ** -0.5, 0.25),
        "coarse_node_first": noise(streams_of[11], (2 * H, H), (2 * H) ** -0.5, 0.1875),
        "coarse_node_second": noise(streams_of[12], (H, H), H ** -0.5, 0.25),
    }


def layer_norm(values):
    average = lax.optimization_barrier(jnp.mean(values, axis=-1, keepdims=True))
    centred = values - average
    variance = lax.optimization_barrier(jnp.mean(centred * centred, axis=-1, keepdims=True))
    return centred * lax.rsqrt(variance + 1e-05)

def message_pass(node_rows, other_part, edge_first, edge_second, node_first, node_second):
    channels = node_rows.shape[1]
    self_part = jnp.dot(node_rows, edge_first[:channels], preferred_element_type=jnp.float32)
    preact = self_part[:, None, :] + other_part
    hidden = jax.nn.silu(preact).astype(jnp.bfloat16)
    messages = jnp.dot(hidden.reshape(-1, channels), edge_second, preferred_element_type=jnp.float32)
    aggregate = lax.optimization_barrier(jnp.sum(messages.reshape(other_part.shape), axis=1)).astype(jnp.bfloat16)
    node_pre = jnp.dot(node_rows, node_first[:channels], preferred_element_type=jnp.float32)
    node_pre = node_pre + jnp.dot(aggregate, node_first[channels:], preferred_element_type=jnp.float32)
    node_hidden = jax.nn.silu(node_pre).astype(jnp.bfloat16)
    update = jnp.dot(node_hidden, node_second, preferred_element_type=jnp.float32)
    return (node_rows.astype(jnp.float32) + layer_norm(update)).astype(jnp.bfloat16)

def reference(features, send_rows, neighbors, membership, coarse_links, edge_first, edge_second, node_first, node_second, coarse_edge_first, coarse_edge_second, coarse_node_first, coarse_node_second):
    channels = features.shape[1]
    blocks = features.reshape(N_DOM, N_DEV, channels)
    row_ids = send_rows.reshape(N_DOM, 2, HALO)
    upward = jax.vmap(lambda node_block, chosen: node_block[chosen])(blocks, row_ids[:, 0])
    downward = jax.vmap(lambda node_block, chosen: node_block[chosen])(blocks, row_ids[:, 1])
    zeros_pad = jnp.zeros((1, HALO, channels), features.dtype)
    from_below = jnp.concatenate([zeros_pad, upward[:-1]], axis=0)
    from_above = jnp.concatenate([downward[1:], zeros_pad], axis=0)
    links = neighbors.reshape(N_DOM, N_DEV, DEG)

    def fine_block(packed):
        node_block, below, above, block_links = packed
        extended = jnp.concatenate([node_block, below, above], axis=0)
        projected = jnp.dot(extended, edge_first[channels:], preferred_element_type=jnp.float32)
        return message_pass(node_block, projected[block_links], edge_first, edge_second, node_first, node_second)
    updated = lax.map(fine_block, (blocks, from_below, from_above, links)).reshape(NODES, channels)
    totals = jax.ops.segment_sum(updated.astype(jnp.float32), membership, num_segments=CLUSTERS)
    counts = jax.ops.segment_sum(jnp.ones((NODES,), jnp.float32), membership, num_segments=CLUSTERS)
    coarse = (totals / counts[:, None]).astype(jnp.bfloat16)
    sources = coarse[coarse_links.reshape(-1)]
    other_part = jnp.dot(sources, coarse_edge_first[channels:], preferred_element_type=jnp.float32)
    other_part = other_part.reshape(CLUSTERS, CDEG, channels)
    coarse_new = message_pass(coarse, other_part, coarse_edge_first, coarse_edge_second, coarse_node_first, coarse_node_second)
    result = updated.astype(jnp.float32) + coarse_new[membership].astype(jnp.float32)
    return result.astype(jnp.bfloat16)
```

```python
import jax
import jax.numpy as jnp
from jax import lax
from jax.experimental import pallas as pl
from jax.experimental.pallas import tpu as pltpu
from jax.sharding import PartitionSpec as P

H = 512
ROWS = 1024
HALO = 128
OWNED = 64
CHIP = 128
TILE = 256
WIDE = H + 128
DOM = 32
F32 = jnp.float32
BF16 = jnp.bfloat16

SIBLING = [(i, i ^ 1) for i in range(DOM)]
ACROSS = [(i, (i + 1) % DOM if i % 2 else (i - 1) % DOM) for i in range(DOM)]


def sibling(value):
    return lax.ppermute(value, "dom", SIBLING)


def across(value):
    return lax.ppermute(value, "dom", ACROSS)


def dot(a, b):
    return jnp.dot(a, b, preferred_element_type=F32)


def gated(half):
    return half + half * jnp.tanh(half)


def columns(ids, span):
    spread = jnp.transpose(jnp.broadcast_to(ids, (128, 128)))
    lane = lax.broadcasted_iota(jnp.int32, (128, 128), 1)
    return jnp.concatenate(
        [(spread == lane + 128 * j).astype(F32).astype(BF16) for j in range(span // 128)], axis=1
    )


def layer_norm(values):
    average = jnp.mean(values, axis=-1, keepdims=True)
    centred = values - average
    variance = jnp.mean(centred * centred, axis=-1, keepdims=True)
    return centred * lax.rsqrt(variance + 1e-05)


def node_update(rows, total, edge_second, node_first, node_second):
    aggregate = dot(total.astype(BF16), edge_second).astype(BF16)
    pre = dot(rows, node_first[:H, :]) + dot(aggregate, node_first[H:, :])
    hidden = gated(0.5 * pre).astype(BF16)
    return (rows.astype(F32) + layer_norm(dot(hidden, node_second))).astype(BF16)


def halo_body(features, send_rows, near, far):
    core = lax.rem(lax.axis_index("dom"), 2)
    up, down = send_rows[0:1, :], send_rows[1:2, :]
    to_sibling = jnp.where(core == 0, up, down)
    to_across = jnp.where(core == 0, down, up)
    near[...] = dot(columns(to_sibling, ROWS), features[...]).astype(BF16)
    far[...] = dot(columns(to_across, ROWS), features[...]).astype(BF16)


def fine_body(
    features, near, far, neighbors, membership, edge_first, edge_second, node_first, node_second,
    updated, first, base, own, projected, pooled,
):
    device = lax.axis_index("dom")
    core = lax.rem(device, 2)
    other = edge_first[H:, :]
    projected[0:ROWS, :] = (0.5 * dot(features[...], other)).astype(BF16)
    below = jnp.where(core == 0, far[...], near[...])
    above = jnp.where(core == 0, near[...], far[...])
    halo = jnp.concatenate([below, above], axis=0)
    projected[ROWS:, :] = (0.5 * dot(halo, other)).astype(BF16)

    for tile in range(ROWS // TILE):
        here = slice(tile * TILE, (tile + 1) * TILE)
        rows = features[here, :]
        self_part = 0.5 * dot(rows, edge_first[:H, :])
        total = jnp.zeros((TILE, H), F32)
        for k in range(4):
            chosen = jnp.concatenate(
                [
                    columns(neighbors[k : k + 1, tile * TILE + s : tile * TILE + s + 128], ROWS + 2 * HALO)
                    for s in range(0, TILE, 128)
                ],
                axis=0,
            )
            total = total + gated(self_part + dot(chosen, projected[...]))
        updated[here, :] = node_update(rows, total, edge_second[...], node_first, node_second[...])

    target = (device - 2) * OWNED + lax.broadcasted_iota(jnp.int32, (5 * OWNED, 128), 0)
    belongs = jnp.concatenate(
        [(membership[j : j + 1, :] == target).astype(F32).astype(BF16) for j in range(ROWS // 128)], axis=1
    )
    pooled[:, :H] = dot(belongs, updated[...])
    count = dot(belongs, jnp.ones((ROWS, 128), BF16))
    high = jnp.floor(count * (1.0 / 64.0))
    lane = lax.broadcasted_iota(jnp.int32, (5 * OWNED, 128), 1)
    pooled[:, H:] = jnp.where(lane < 64, high, count - 64.0 * high)
    first[...] = pooled[pl.ds(pl.multiple_of((1 - core) * 256, 64), OWNED), :].astype(BF16)
    base[...] = pooled[pl.ds(pl.multiple_of(core * 192, 64), CHIP), :].astype(BF16)
    own[...] = pooled[pl.ds(pl.multiple_of(128 - 64 * core, 64), CHIP), :].astype(BF16)


def coarse_body(
    coarse, near, far, links, edge_first, edge_second, node_first, node_second, updated, projected
):
    device = lax.axis_index("dom")
    core = lax.rem(device, 2)
    start = (lax.div(device, 2) - 1) * CHIP
    below = jnp.where(core == 0, far[...], near[...])
    above = jnp.where(core == 0, near[...], far[...])
    rows = coarse[...]
    lookup = jnp.concatenate([below, rows, above], axis=0)
    projected[...] = (0.5 * dot(lookup, edge_first[H:, :])).astype(BF16)
    self_part = 0.5 * dot(rows, edge_first[:H, :])
    total = jnp.zeros((CHIP, H), F32)
    for k in range(8):
        chosen = columns(links[k : k + 1, :] - start, 3 * CHIP)
        total = total + gated(self_part + dot(chosen, projected[...]))
    updated[...] = node_update(rows, total, edge_second[...], node_first, node_second[...])


def unpool_body(fine, coarse, near, far, membership, result):
    device = lax.axis_index("dom")
    core = lax.rem(device, 2)
    start = (lax.div(device, 2) - 1) * CHIP
    below = jnp.where(core == 0, far[...], near[...])
    above = jnp.where(core == 0, near[...], far[...])
    lookup = jnp.concatenate([below, coarse[...], above], axis=0)
    for j in range(ROWS // 128):
        here = slice(j * 128, (j + 1) * 128)
        chosen = columns(membership[j : j + 1, :] - start, 3 * CHIP)
        result[here, :] = (fine[here, :].astype(F32) + dot(chosen, lookup)).astype(BF16)


def call(body, outs, scratch, flops, *args):
    return pl.pallas_call(
        body,
        out_shape=[jax.ShapeDtypeStruct(shape, BF16) for shape in outs],
        in_specs=[pl.BlockSpec(memory_space=pltpu.VMEM)] * len(args),
        out_specs=[pl.BlockSpec(memory_space=pltpu.VMEM)] * len(outs),
        scratch_shapes=scratch,
        compiler_params=pltpu.CompilerParams(vmem_limit_bytes=40 * 1024 * 1024),
        cost_estimate=pl.CostEstimate(flops=flops, bytes_accessed=4 * 1024 * 1024, transcendentals=0),
    )(*args)


def shards(
    features,
    send_rows,
    neighbors,
    membership,
    coarse_links,
    edge_first,
    edge_second,
    node_first,
    node_second,
    coarse_edge_first,
    coarse_edge_second,
    coarse_node_first,
    coarse_node_second,
):
    core = lax.rem(lax.axis_index("dom"), 2)
    members = membership.reshape(ROWS // 128, 128)
    near, far = call(halo_body, [(HALO, H)] * 2, [], 300000000, features, send_rows)
    near, far = sibling(near), across(far)
    my_links = coarse_links.T
    their_links = sibling(my_links)
    links = jnp.where(
        core == 0,
        jnp.concatenate([my_links, their_links], axis=1),
        jnp.concatenate([their_links, my_links], axis=1),
    )
    updated, first, base, own = call(
        fine_body,
        [(ROWS, H), (OWNED, WIDE), (CHIP, WIDE), (CHIP, WIDE)],
        [pltpu.VMEM((ROWS + 2 * HALO, H), BF16), pltpu.VMEM((5 * OWNED, WIDE), F32)],
        9000000000,
        features, near, far, neighbors.T, members, edge_first, edge_second, node_first, node_second,
    )
    first = sibling(first).astype(F32)
    nothing = jnp.zeros_like(first)
    extra = jnp.where(
        core == 0, jnp.concatenate([nothing, first], axis=0), jnp.concatenate([first, nothing], axis=0)
    )
    arrived = across((base.astype(F32) + extra).astype(BF16))
    mine = (own.astype(F32) + arrived.astype(F32)).astype(BF16)
    theirs = sibling(mine)
    sums = mine.astype(F32) + theirs.astype(F32)
    counts = 64.0 * sums[:, H : H + 1] + sums[:, H + 64 : H + 65]
    coarse = (sums[:, :H] / counts).astype(BF16)

    far = across(coarse)
    near = sibling(far)
    (coarse_new,) = call(
        coarse_body,
        [(CHIP, H)],
        [pltpu.VMEM((3 * CHIP, H), BF16)],
        1000000000,
        coarse, near, far, links, coarse_edge_first, coarse_edge_second, coarse_node_first, coarse_node_second,
    )
    far = across(coarse_new)
    near = sibling(far)
    (result,) = call(unpool_body, [(ROWS, H)], [], 400000000, updated, coarse_new, near, far, members)
    return result


def solution(mesh):
    placed = (
        P(("grp", "dom"), None),
        P(("grp", "dom"), None),
        P(("grp", "dom"), None),
        P(("grp", "dom")),
        P(("grp", "dom"), None),
        P(),
        P(),
        P(),
        P(),
        P(),
        P(),
        P(),
        P(),
    )
    return jax.shard_map(
        shards, mesh=mesh, in_specs=placed, out_specs=P(("grp", "dom"), None), check_vma=False
    )
```

```python
import jax
import jax.numpy as jnp
from jax import lax
from jax.experimental import pallas as pl
from jax.experimental.pallas import tpu as pltpu
from jax.sharding import PartitionSpec as P

H = 512
ROWS = 1024
HALO = 128
OWNED = 64
CHIP = 128
TILE = 512
WIDE = H + 128
DOM = 32
F32 = jnp.float32
BF16 = jnp.bfloat16

SIBLING = [(i, i ^ 1) for i in range(DOM)]


def facing(parts):
    pairs = []
    for part in range(parts):
        other = part ^ 1 if (part ^ 1) < parts else part
        for i in range(DOM):
            j = i + 1 if i % 2 else i - 1
            pairs.append((part * DOM + i, part * DOM + j if 0 <= j < DOM else other * DOM + i))
    return pairs


def sibling(value):
    return lax.ppermute(value, "dom", SIBLING)


def across(value):
    return lax.ppermute(value, ("grp", "dom"), facing(lax.axis_size("grp")))


def dot(a, b):
    return jnp.dot(a, b, preferred_element_type=F32)


def gated(half):
    return half + half * jnp.tanh(half)


def columns(ids, span):
    spread = jnp.transpose(jnp.broadcast_to(ids, (128, 128))).astype(jnp.int16)
    lane = lax.broadcasted_iota(jnp.int32, (128, 128), 1).astype(jnp.int16)
    one, zero = jnp.ones((), BF16), jnp.zeros((), BF16)
    return jnp.concatenate(
        [jnp.where(spread == lane + jnp.int16(128 * j), one, zero) for j in range(span // 128)], axis=1
    )


def layer_norm(values):
    average = jnp.mean(values, axis=-1, keepdims=True)
    centred = values - average
    variance = jnp.mean(centred * centred, axis=-1, keepdims=True)
    return centred * lax.rsqrt(variance + 1e-05)


def node_update(rows, node_part, total, edge_second, node_other, node_second):
    aggregate = dot(total.astype(BF16), edge_second).astype(BF16)
    hidden = gated(node_part + 0.5 * dot(aggregate, node_other)).astype(BF16)
    return (rows.astype(F32) + layer_norm(dot(hidden, node_second))).astype(BF16)


def pieces(source, target, arrived, count):
    step = source.shape[0] // count
    return [
        pltpu.make_async_copy(source.at[pl.ds(j * step, step), :], target.at[pl.ds(j * step, step), :], arrived.at[j])
        for j in range(count)
    ]


def halo_body(features, send_rows, edge_first, held, edge_held, near, far, ids, ids_arrived, arrived, edge_arrived):
    core = lax.rem(lax.axis_index("dom"), 2)
    ids_copy = pltpu.make_async_copy(send_rows, ids, ids_arrived)
    ids_copy.start()
    copies = pieces(features, held, arrived, 4)
    edge_copies = pieces(edge_first, edge_held, edge_arrived, 4)
    for copy in copies + edge_copies:
        copy.start()
    ids_copy.wait()
    up, down = ids[0:1, :], ids[1:2, :]
    chosen = jnp.concatenate(
        [columns(jnp.where(core == 0, up, down), ROWS), columns(jnp.where(core == 0, down, up), ROWS)], axis=0
    )
    for copy in copies:
        copy.wait()
    rows = dot(chosen, held[...]).astype(BF16)
    near[...] = rows[:HALO, :]
    far[...] = rows[HALO:, :]
    for copy in edge_copies:
        copy.wait()


def local_body(features, neighbors, edge_first, node_first, projected, self_part, early, node_part, node_self, arrived):
    copy = pltpu.make_async_copy(node_first.at[pl.ds(0, H), :], node_self, arrived)
    copy.start()
    projected[...] = (0.5 * dot(features[...], edge_first[H:, :])).astype(BF16)
    self_part[...] = 0.5 * dot(features[...], edge_first[:H, :])
    chosen = jnp.concatenate([columns(neighbors[0:1, s : s + 128], ROWS) for s in range(0, ROWS, 128)], axis=0)
    early[...] = self_part[...] + dot(chosen, projected[...])
    copy.wait()
    node_part[...] = 0.5 * dot(features[...], node_self[...])


def pool(target, membership, updated):
    belongs = jnp.concatenate(
        [
            jnp.where(membership[j : j + 1, :] == target, jnp.ones((), F32), jnp.zeros((), F32)).astype(BF16)
            for j in range(ROWS // 128)
        ],
        axis=1,
    )
    count = dot(belongs, jnp.ones((ROWS, 128), BF16))
    high = jnp.floor(count * (1.0 / 64.0))
    lane = lax.broadcasted_iota(jnp.int32, count.shape, 1)
    return dot(belongs, updated).astype(BF16), jnp.where(lane < 64, high, count - 64.0 * high).astype(BF16)


def fine_body(
    features, local, self_part, early, node_part, near, far, neighbors, membership,
    edge_first, edge_second, node_first, node_second,
    updated, first,
    projected, second, node_other, last, arrived,
):
    copies = [
        pltpu.make_async_copy(edge_second, second, arrived.at[0]),
        pltpu.make_async_copy(node_first.at[pl.ds(H, H), :], node_other, arrived.at[1]),
        pltpu.make_async_copy(node_second, last, arrived.at[2]),
    ]
    for copy in copies:
        copy.start()
    device = lax.axis_index("dom")
    core = lax.rem(device, 2)
    projected[0:ROWS, :] = local[...]
    below = jnp.where(core == 0, far[...], near[...])
    above = jnp.where(core == 0, near[...], far[...])
    halo = jnp.concatenate([below, above], axis=0)
    projected[ROWS:, :] = (0.5 * dot(halo, edge_first[H:, :])).astype(BF16)

    for tile in range(ROWS // TILE):
        here = slice(tile * TILE, (tile + 1) * TILE)
        spans = range(tile * TILE, (tile + 1) * TILE, 128)
        chosen = jnp.concatenate(
            [columns(neighbors[0:1, s : s + 128] - ROWS, 2 * HALO) for s in spans], axis=0
        )
        total = gated(early[here, :] + dot(chosen, projected[ROWS:, :]))
        for k in range(1, 4):
            chosen = jnp.concatenate(
                [columns(neighbors[k : k + 1, s : s + 128], ROWS + 2 * HALO) for s in spans], axis=0
            )
            total = total + gated(self_part[here, :] + dot(chosen, projected[...]))
        if tile == 0:
            for copy in copies:
                copy.wait()
        updated[here, :] = node_update(
            features[here, :], node_part[here, :], total, second[...], node_other[...], last[...]
        )

    target = (device + 2 - 4 * core) * OWNED + lax.broadcasted_iota(jnp.int32, (OWNED, 128), 0)
    first[:, :H], first[:, H:] = pool(target, membership, updated[...])

def pool_body(updated, membership, base, own):
    device = lax.axis_index("dom")
    core = lax.rem(device, 2)
    row = lax.broadcasted_iota(jnp.int32, (CHIP, 128), 0)
    target = jnp.concatenate([(device - 2 + 3 * core) * OWNED + row, (device - core) * OWNED + row], axis=0)
    sums, counts = pool(target, membership, updated[...])
    base[:, :H], base[:, H:] = sums[:CHIP, :], counts[:CHIP, :]
    own[:, :H], own[:, H:] = sums[CHIP:, :], counts[CHIP:, :]


def own_body(
    coarse, links, edge_first, node_first, edge_second, node_second,
    early, self_part, node_part, edge_held, node_held, arrived,
):
    copies = [
        pltpu.make_async_copy(edge_second, edge_held, arrived.at[0]),
        pltpu.make_async_copy(node_second, node_held, arrived.at[1]),
    ]
    for copy in copies:
        copy.start()
    start = lax.div(lax.axis_index("dom"), 2) * CHIP
    rows = coarse[...]
    projected = (0.5 * dot(rows, edge_first[H:, :])).astype(BF16)
    self_part[...] = 0.5 * dot(rows, edge_first[:H, :])
    node_part[...] = 0.5 * dot(rows, node_first[:H, :])
    chosen = jnp.concatenate([columns(links[k : k + 1, :] - start, CHIP) for k in range(8)], axis=0)
    early[...] = dot(chosen, projected)
    for copy in copies:
        copy.wait()


def far_body(early, far, links, edge_first, other):
    device = lax.axis_index("dom")
    start = (lax.div(device, 2) - 1 + 2 * lax.rem(device, 2)) * CHIP
    projected = (0.5 * dot(far[...], edge_first[H:, :])).astype(BF16)
    chosen = jnp.concatenate([columns(links[k : k + 1, :] - start, CHIP) for k in range(8)], axis=0)
    other[...] = early[...] + dot(chosen, projected)


def coarse_body(
    coarse, early, self_part, node_part, near, links, edge_first, edge_second, node_first, node_second, updated
):
    device = lax.axis_index("dom")
    start = (lax.div(device, 2) + 1 - 2 * lax.rem(device, 2)) * CHIP
    projected = (0.5 * dot(near[...], edge_first[H:, :])).astype(BF16)
    chosen = jnp.concatenate([columns(links[k : k + 1, :] - start, CHIP) for k in range(8)], axis=0)
    other = early[...] + dot(chosen, projected)
    total = jnp.zeros((CHIP, H), F32)
    for k in range(8):
        total = total + gated(self_part[...] + other[k * CHIP : (k + 1) * CHIP, :])
    updated[...] = node_update(
        coarse[...], node_part[...], total, edge_second[...], node_first[H:, :], node_second[...]
    )


def spread_body(fine, coarse, membership, partial, far_rows, near_rows):
    device = lax.axis_index("dom")
    core = lax.rem(device, 2)
    chip = lax.div(device, 2)
    for j in range(ROWS // 256):
        here = slice(j * 256, (j + 1) * 256)

        def rows_of(which):
            return jnp.concatenate(
                [columns(membership[2 * j + i : 2 * j + i + 1, :] - which * CHIP, CHIP) for i in range(2)], axis=0
            )

        partial[here, :] = fine[here, :].astype(F32) + dot(rows_of(chip), coarse[...])
        far_rows[here, :] = rows_of(chip - 1 + 2 * core)
        near_rows[here, :] = rows_of(chip + 1 - 2 * core)


def unpool_body(partial, far_rows, near_rows, far, near, result, made, sent):
    lookup = jnp.concatenate([far[...], near[...]], axis=0)
    copies = []
    for j in range(ROWS // 256):
        here = slice(j * 256, (j + 1) * 256)
        chosen = jnp.concatenate([far_rows[here, :], near_rows[here, :]], axis=1)
        made[here, :] = (partial[here, :] + dot(chosen, lookup)).astype(BF16)
        copy = pltpu.make_async_copy(
            made.at[pl.ds(j * 256, 256), :], result.at[pl.ds(j * 256, 256), :], sent.at[j]
        )
        copy.start()
        copies.append(copy)
    for copy in copies:
        copy.wait()


VMEM = pl.BlockSpec(memory_space=pltpu.VMEM)
ANY = pl.BlockSpec(memory_space=pltpu.HBM)


def call(body, outs, scratch, flops, args, apart=(), out_spec=VMEM):
    args = [pltpu.with_memory_space_constraint(a, pltpu.HBM) if i in apart else a for i, a in enumerate(args)]
    return pl.pallas_call(
        body,
        out_shape=[jax.ShapeDtypeStruct(shape, kind) for shape, kind in outs],
        in_specs=[ANY if i in apart else VMEM for i in range(len(args))],
        out_specs=[out_spec] * len(outs),
        scratch_shapes=scratch,
        compiler_params=pltpu.CompilerParams(vmem_limit_bytes=24 * 1024 * 1024),
        cost_estimate=pl.CostEstimate(flops=flops, bytes_accessed=4 * 1024 * 1024, transcendentals=0),
    )(*args)


def halo_rows(*args):
    return call(
        halo_body,
        [((ROWS, H), BF16), ((2 * H, H), BF16), ((HALO, H), BF16), ((HALO, H), BF16)],
        [
            pltpu.VMEM((2, HALO), jnp.int32),
            pltpu.SemaphoreType.DMA(()),
            pltpu.SemaphoreType.DMA((4,)),
            pltpu.SemaphoreType.DMA((4,)),
        ],
        300000000,
        args,
        (0, 1, 2),
    )


def local_parts(*args):
    return call(
        local_body,
        [((ROWS, H), BF16), ((ROWS, H), F32), ((ROWS, H), F32), ((ROWS, H), F32)],
        [pltpu.VMEM((H, H), BF16), pltpu.SemaphoreType.DMA(())],
        2600000000,
        args,
        (3,),
    )


def fine_stage(*args):
    return call(
        fine_body,
        [((ROWS, H), BF16), ((OWNED, WIDE), BF16)],
        [
            pltpu.VMEM((ROWS + 2 * HALO, H), BF16),
            pltpu.VMEM((H, H), BF16),
            pltpu.VMEM((H, H), BF16),
            pltpu.VMEM((H, H), BF16),
            pltpu.SemaphoreType.DMA((3,)),
        ],
        7000000000,
        args,
        (10, 11, 12),
    )


def pooled(*args):
    return call(pool_body, [((CHIP, WIDE), BF16), ((CHIP, WIDE), BF16)], [], 400000000, args)


def own_parts(*args):
    return call(
        own_body,
        [((8 * CHIP, H), F32), ((CHIP, H), F32), ((CHIP, H), F32), ((H, H), BF16), ((H, H), BF16)],
        [pltpu.SemaphoreType.DMA((2,))],
        400000000,
        args,
        (4, 5),
    )


def far_parts(*args):
    return call(far_body, [((8 * CHIP, H), F32)], [], 200000000, args)[0]


def coarse_stage(*args):
    return call(coarse_body, [((CHIP, H), BF16)], [], 1000000000, args)[0]


def spread(*args):
    return call(spread_body, [((ROWS, H), F32), ((ROWS, CHIP), BF16), ((ROWS, CHIP), BF16)], [], 400000000, args)


def unpooled(*args):
    return call(
        unpool_body,
        [((ROWS, H), BF16)],
        [pltpu.VMEM((ROWS, H), BF16), pltpu.SemaphoreType.DMA((4,))],
        400000000,
        args,
        (),
        ANY,
    )[0]


def shards(
    features,
    send_rows,
    neighbors,
    membership,
    coarse_links,
    edge_first,
    edge_second,
    node_first,
    node_second,
    coarse_edge_first,
    coarse_edge_second,
    coarse_node_first,
    coarse_node_second,
):
    core = lax.rem(lax.axis_index("dom"), 2)
    members = membership.reshape(ROWS // 128, 128)
    my_links = coarse_links.T
    their_links = sibling(my_links)
    held, edge_held, near, far = halo_rows(features, send_rows, edge_first)
    near, far = sibling(near), across(far)
    projected, self_part, early, node_part = local_parts(held, neighbors.T, edge_held, node_first)
    near, far, their_links = lax.optimization_barrier((near, far, their_links))
    updated, first = fine_stage(
        held, projected, self_part, early, node_part, near, far, neighbors.T, members,
        edge_held, edge_second, node_first, node_second,
    )
    links = jnp.where(
        core == 0,
        jnp.concatenate([my_links, their_links], axis=1),
        jnp.concatenate([their_links, my_links], axis=1),
    )
    first = sibling(first)
    base, own = pooled(updated, members)
    nothing = jnp.zeros_like(first)
    extra = jnp.where(
        core == 0, jnp.concatenate([nothing, first], axis=0), jnp.concatenate([first, nothing], axis=0)
    ).astype(F32)
    arrived = across((base.astype(F32) + extra).astype(BF16))
    mine = (own.astype(F32) + arrived.astype(F32)).astype(BF16)
    theirs = sibling(mine)
    sums = mine.astype(F32) + theirs.astype(F32)
    counts = 64.0 * sums[:, H : H + 1] + sums[:, H + 64 : H + 65]
    coarse = (sums[:, :H] / counts).astype(BF16)

    far = across(coarse)
    early, self_part, node_part, edge_held, node_held = lax.optimization_barrier(
        own_parts(coarse, links, coarse_edge_first, coarse_node_first, coarse_edge_second, coarse_node_second)
    )
    far, early = lax.optimization_barrier((far, early))
    near = sibling(far)
    early = far_parts(early, far, links, coarse_edge_first)
    coarse_new = coarse_stage(
        coarse, early, self_part, node_part, near, links, coarse_edge_first, edge_held, coarse_node_first, node_held
    )
    far = across(coarse_new)
    partial, far_rows, near_rows = spread(updated, coarse_new, members)
    far, partial = lax.optimization_barrier((far, partial))
    near = sibling(far)
    return unpooled(partial, far_rows, near_rows, far, near)


def solution(mesh):
    placed = (
        P(("grp", "dom"), None),
        P(("grp", "dom"), None),
        P(("grp", "dom"), None),
        P(("grp", "dom")),
        P(("grp", "dom"), None),
        P(),
        P(),
        P(),
        P(),
        P(),
        P(),
        P(),
        P(),
    )
    return jax.shard_map(
        shards, mesh=mesh, in_specs=placed, out_specs=P(("grp", "dom"), None), check_vma=False
    )
```

```python
import jax
import jax.numpy as jnp
from jax import lax
from jax.experimental import pallas as pl
from jax.experimental.pallas import tpu as pltpu
from jax.sharding import PartitionSpec as P

H = 512
ROWS = 1024
HALO = 128
OWNED = 64
CHIP = 128
TILE = 512
PACK = 2 * CHIP + 16
DOM = 32
F32 = jnp.float32
BF16 = jnp.bfloat16

SIBLING = [(i, i ^ 1) for i in range(DOM)]


def facing(parts, step):
    pairs = []
    for part in range(parts):
        other = part ^ 1 if (part ^ 1) < parts else part
        for i in range(DOM):
            j = i + 2 * step - 1 if i % 2 else i - 2 * step + 1
            pairs.append((part * DOM + i, part * DOM + j if 0 <= j < DOM else other * DOM + i))
    return pairs


def sibling(value):
    return lax.ppermute(value, "dom", SIBLING)


def across(value, step=1):
    return lax.ppermute(value, ("grp", "dom"), facing(lax.axis_size("grp"), step))


def place():
    device = lax.axis_index("dom")
    core = lax.rem(device, 2)
    chip = lax.div(device, 2)
    return core, chip, chip - 1 + 2 * core, chip + 1 - 2 * core


def dot(a, b):
    return jnp.dot(a, b, preferred_element_type=F32)


def gated(half):
    return half + half * jnp.tanh(half)


def columns(ids, span):
    spread = jnp.transpose(jnp.broadcast_to(ids, (128, 128))).astype(jnp.int16)
    lane = lax.broadcasted_iota(jnp.int32, (128, 128), 1).astype(jnp.int16)
    one, zero = jnp.ones((), BF16), jnp.zeros((), BF16)
    return jnp.concatenate(
        [jnp.where(spread == lane + jnp.int16(128 * j), one, zero) for j in range(span // 128)], axis=1
    )


def layer_norm(values):
    average = jnp.mean(values, axis=-1, keepdims=True)
    centred = values - average
    variance = jnp.mean(centred * centred, axis=-1, keepdims=True)
    return centred * lax.rsqrt(variance + 1e-05)


def node_update(rows, node_part, total, edge_second, node_other, node_second):
    aggregate = dot(total.astype(BF16), edge_second).astype(BF16)
    hidden = gated(node_part + 0.5 * dot(aggregate, node_other)).astype(BF16)
    return (rows.astype(F32) + layer_norm(dot(hidden, node_second))).astype(BF16)


def pieces(source, target, arrived, count):
    step = source.shape[0] // count
    return [
        pltpu.make_async_copy(source.at[pl.ds(j * step, step), :], target.at[pl.ds(j * step, step), :], arrived.at[j])
        for j in range(count)
    ]


def halo_body(features, send_rows, edge_first, held, edge_held, near, far, ids, ids_arrived, arrived, edge_arrived):
    core = lax.rem(lax.axis_index("dom"), 2)
    ids_copy = pltpu.make_async_copy(send_rows, ids, ids_arrived)
    ids_copy.start()
    copies = pieces(features, held, arrived, 4)
    edge_copies = pieces(edge_first, edge_held, edge_arrived, 4)
    for copy in copies + edge_copies:
        copy.start()
    ids_copy.wait()
    up, down = ids[0:1, :], ids[1:2, :]
    chosen = jnp.concatenate(
        [columns(jnp.where(core == 0, up, down), ROWS), columns(jnp.where(core == 0, down, up), ROWS)], axis=0
    )
    for copy in copies:
        copy.wait()
    rows = dot(chosen, held[...]).astype(BF16)
    near[...] = rows[:HALO, :]
    far[...] = rows[HALO:, :]
    for copy in edge_copies:
        copy.wait()


def local_body(features, neighbors, edge_first, node_first, projected, self_part, early, node_part, node_self, arrived):
    copy = pltpu.make_async_copy(node_first.at[pl.ds(0, H), :], node_self, arrived)
    copy.start()
    projected[...] = (0.5 * dot(features[...], edge_first[H:, :])).astype(BF16)
    self_part[...] = 0.5 * dot(features[...], edge_first[:H, :])
    chosen = jnp.concatenate([columns(neighbors[0:1, s : s + 128], ROWS) for s in range(0, ROWS, 128)], axis=0)
    early[...] = self_part[...] + dot(chosen, projected[...])
    copy.wait()
    node_part[...] = 0.5 * dot(features[...], node_self[...])


def pool(chips, membership, updated):
    row = lax.broadcasted_iota(jnp.int32, (CHIP, 128), 0)
    target = jnp.concatenate([chip * CHIP + row for chip in chips], axis=0)
    belongs = jnp.concatenate(
        [
            jnp.where(membership[j : j + 1, :] == target, jnp.ones((), F32), jnp.zeros((), F32)).astype(BF16)
            for j in range(ROWS // 128)
        ],
        axis=1,
    )
    count = lax.dot_general(
        jnp.ones((16, ROWS), BF16), belongs, (((1,), (1,)), ((), ())), preferred_element_type=F32
    )
    high = jnp.floor(count * (1.0 / 64.0))
    digit = lax.broadcasted_iota(jnp.int32, count.shape, 0)
    return dot(belongs, updated).astype(BF16), jnp.where(digit == 0, high, count - 64.0 * high).astype(BF16)


def divided(sums, count):
    whole = jnp.maximum(64.0 * count[0:1, :] + count[1:2, :], 1.0)
    column = jnp.transpose(jnp.broadcast_to(whole, (CHIP, 128)))
    return (sums / jnp.concatenate([column] * (H // 128), axis=1)).astype(BF16)


def fine_body(
    features, local, self_part, early, node_part, near, far, neighbors, membership,
    edge_first, edge_second, node_first, node_second,
    updated, first,
    projected, second, node_other, last, arrived,
):
    copies = [
        pltpu.make_async_copy(edge_second, second, arrived.at[0]),
        pltpu.make_async_copy(node_first.at[pl.ds(H, H), :], node_other, arrived.at[1]),
        pltpu.make_async_copy(node_second, last, arrived.at[2]),
    ]
    for copy in copies:
        copy.start()
    device = lax.axis_index("dom")
    core = lax.rem(device, 2)
    projected[0:ROWS, :] = local[...]
    below = jnp.where(core == 0, far[...], near[...])
    above = jnp.where(core == 0, near[...], far[...])
    halo = jnp.concatenate([below, above], axis=0)
    projected[ROWS:, :] = (0.5 * dot(halo, edge_first[H:, :])).astype(BF16)

    for tile in range(ROWS // TILE):
        here = slice(tile * TILE, (tile + 1) * TILE)
        spans = range(tile * TILE, (tile + 1) * TILE, 128)
        chosen = jnp.concatenate(
            [columns(neighbors[0:1, s : s + 128] - ROWS, 2 * HALO) for s in spans], axis=0
        )
        total = gated(early[here, :] + dot(chosen, projected[ROWS:, :]))
        for k in range(1, 4):
            chosen = jnp.concatenate(
                [columns(neighbors[k : k + 1, s : s + 128], ROWS + 2 * HALO) for s in spans], axis=0
            )
            total = total + gated(self_part[here, :] + dot(chosen, projected[...]))
        if tile == 0:
            for copy in copies:
                copy.wait()
        updated[here, :] = node_update(
            features[here, :], node_part[here, :], total, second[...], node_other[...], last[...]
        )

    _, chip, _, near_chip = place()
    first[: 2 * CHIP, :], counts = pool((near_chip, chip), membership, updated[...])
    first[2 * CHIP :, :] = jnp.concatenate([counts, jnp.zeros((16, H - 2 * CHIP), BF16)], axis=1)


def keep_body(updated, membership, first, keep):
    _, _, far_chip, _ = place()
    keep[:CHIP, :], counts = pool((far_chip,), membership, updated[...])
    keep[CHIP:, :] = first[CHIP:, :]
    keep[2 * CHIP :, :CHIP] = counts


def totals_body(mine, one, two, passed):
    core, chip, _, _ = place()
    reach = jnp.where(core == 0, chip, DOM // 2 - 1 - chip)
    has_one = jnp.where(reach >= 1, 1.0, 0.0)
    has_two = jnp.where(reach >= 2, 1.0, 0.0)
    counts = slice(2 * CHIP, PACK)
    sums = mine[:CHIP, :].astype(F32) + has_one * one[CHIP : 2 * CHIP, :].astype(F32)
    sums = sums + has_two * two[:CHIP, :].astype(F32)
    count = mine[counts, :CHIP].astype(F32) + has_one * one[counts, CHIP : 2 * CHIP].astype(F32)
    count = count + has_two * two[CHIP:, :CHIP].astype(F32)
    passed[:CHIP, :] = divided(sums, count)
    passed[CHIP : 2 * CHIP, :] = (has_one * one[:CHIP, :].astype(F32)).astype(BF16)
    passed[counts, :] = (has_one * one[counts, :].astype(F32)).astype(BF16)


def links_body(
    links, edge_first, edge_second, node_first, node_second,
    own_rows, far_rows, near_rows, edge_first_held, edge_second_held, node_first_held, node_second_held, arrived,
):
    copies = [
        pltpu.make_async_copy(source, target, arrived.at[i])
        for i, (source, target) in enumerate(
            (
                (edge_first, edge_first_held),
                (edge_second, edge_second_held),
                (node_first, node_first_held),
                (node_second, node_second_held),
            )
        )
    ]
    for copy in copies:
        copy.start()
    _, chip, far_chip, near_chip = place()
    for rows, which in ((own_rows, chip), (far_rows, far_chip), (near_rows, near_chip)):
        for k in range(8):
            rows[k * CHIP : (k + 1) * CHIP, :] = columns(links[k : k + 1, :] - which * CHIP, CHIP)
    for copy in copies:
        copy.wait()


def far_body(passed, far_rows, edge_first, other):
    projected = (0.5 * dot(passed[:CHIP, :], edge_first[H:, :])).astype(BF16)
    other[...] = dot(far_rows[...], projected)


def coarse_body(
    mine, passed, got, early, own_rows, near_rows, edge_first, edge_second, node_first, node_second, updated
):
    counts = slice(2 * CHIP, PACK)
    between = passed[CHIP : 2 * CHIP, :].astype(F32) + got[CHIP : 2 * CHIP, :].astype(F32)
    count = passed[counts, :CHIP].astype(F32) + got[counts, :CHIP].astype(F32)
    coarse = divided(
        mine[CHIP : 2 * CHIP, :].astype(F32) + between, mine[counts, CHIP : 2 * CHIP].astype(F32) + count
    )
    self_part = 0.5 * dot(coarse, edge_first[:H, :])
    node_part = 0.5 * dot(coarse, node_first[:H, :])
    both = jnp.concatenate([coarse, got[:CHIP, :]], axis=0)
    projected = (0.5 * dot(both, edge_first[H:, :])).astype(BF16)
    other = early[...] + dot(jnp.concatenate([own_rows[...], near_rows[...]], axis=1), projected)
    total = jnp.zeros((CHIP, H), F32)
    for k in range(8):
        total = total + gated(self_part + other[k * CHIP : (k + 1) * CHIP, :])
    updated[...] = node_update(coarse, node_part, total, edge_second[...], node_first[H:, :], node_second[...])


def spread_body(fine, coarse, membership, partial, far_rows, near_rows):
    device = lax.axis_index("dom")
    core = lax.rem(device, 2)
    chip = lax.div(device, 2)
    for j in range(ROWS // 256):
        here = slice(j * 256, (j + 1) * 256)

        def rows_of(which):
            return jnp.concatenate(
                [columns(membership[2 * j + i : 2 * j + i + 1, :] - which * CHIP, CHIP) for i in range(2)], axis=0
            )

        partial[here, :] = fine[here, :].astype(F32) + dot(rows_of(chip), coarse[...])
        far_rows[here, :] = rows_of(chip - 1 + 2 * core)
        near_rows[here, :] = rows_of(chip + 1 - 2 * core)


def unpool_body(partial, far_rows, near_rows, far, near, result, made, sent):
    lookup = jnp.concatenate([far[...], near[...]], axis=0)
    copies = []
    for j in range(ROWS // 256):
        here = slice(j * 256, (j + 1) * 256)
        chosen = jnp.concatenate([far_rows[here, :], near_rows[here, :]], axis=1)
        made[here, :] = (partial[here, :] + dot(chosen, lookup)).astype(BF16)
        copy = pltpu.make_async_copy(
            made.at[pl.ds(j * 256, 256), :], result.at[pl.ds(j * 256, 256), :], sent.at[j]
        )
        copy.start()
        copies.append(copy)
    for copy in copies:
        copy.wait()


VMEM = pl.BlockSpec(memory_space=pltpu.VMEM)
ANY = pl.BlockSpec(memory_space=pltpu.HBM)


def call(body, outs, scratch, flops, args, apart=(), out_spec=VMEM):
    args = [pltpu.with_memory_space_constraint(a, pltpu.HBM) if i in apart else a for i, a in enumerate(args)]
    return pl.pallas_call(
        body,
        out_shape=[jax.ShapeDtypeStruct(shape, kind) for shape, kind in outs],
        in_specs=[ANY if i in apart else VMEM for i in range(len(args))],
        out_specs=[out_spec] * len(outs),
        scratch_shapes=scratch,
        compiler_params=pltpu.CompilerParams(vmem_limit_bytes=24 * 1024 * 1024),
        cost_estimate=pl.CostEstimate(flops=flops, bytes_accessed=4 * 1024 * 1024, transcendentals=0),
    )(*args)


def halo_rows(*args):
    return call(
        halo_body,
        [((ROWS, H), BF16), ((2 * H, H), BF16), ((HALO, H), BF16), ((HALO, H), BF16)],
        [
            pltpu.VMEM((2, HALO), jnp.int32),
            pltpu.SemaphoreType.DMA(()),
            pltpu.SemaphoreType.DMA((4,)),
            pltpu.SemaphoreType.DMA((4,)),
        ],
        300000000,
        args,
        (0, 1, 2),
    )


def local_parts(*args):
    return call(
        local_body,
        [((ROWS, H), BF16), ((ROWS, H), F32), ((ROWS, H), F32), ((ROWS, H), F32)],
        [pltpu.VMEM((H, H), BF16), pltpu.SemaphoreType.DMA(())],
        2600000000,
        args,
        (3,),
    )


def fine_stage(*args):
    return call(
        fine_body,
        [((ROWS, H), BF16), ((PACK, H), BF16)],
        [
            pltpu.VMEM((ROWS + 2 * HALO, H), BF16),
            pltpu.VMEM((H, H), BF16),
            pltpu.VMEM((H, H), BF16),
            pltpu.VMEM((H, H), BF16),
            pltpu.SemaphoreType.DMA((3,)),
        ],
        7000000000,
        args,
        (10, 11, 12),
    )


def kept(*args):
    return call(keep_body, [((PACK, H), BF16)], [], 200000000, args)[0]


def totals(*args):
    return call(totals_body, [((PACK, H), BF16)], [], 100000000, args)[0]


def link_rows(*args):
    return call(
        links_body,
        [((8 * CHIP, CHIP), BF16)] * 3 + [((2 * H, H), BF16), ((H, H), BF16)] * 2,
        [pltpu.SemaphoreType.DMA((4,))],
        400000000,
        args,
        (1, 2, 3, 4),
    )


def far_parts(*args):
    return call(far_body, [((8 * CHIP, H), F32)], [], 200000000, args)[0]


def coarse_stage(*args):
    return call(coarse_body, [((CHIP, H), BF16)], [], 1000000000, args)[0]


def spread(*args):
    return call(spread_body, [((ROWS, H), F32), ((ROWS, CHIP), BF16), ((ROWS, CHIP), BF16)], [], 400000000, args)


def unpooled(*args):
    return call(
        unpool_body,
        [((ROWS, H), BF16)],
        [pltpu.VMEM((ROWS, H), BF16), pltpu.SemaphoreType.DMA((4,))],
        400000000,
        args,
        (),
        ANY,
    )[0]


def shards(
    features,
    send_rows,
    neighbors,
    membership,
    coarse_links,
    edge_first,
    edge_second,
    node_first,
    node_second,
    coarse_edge_first,
    coarse_edge_second,
    coarse_node_first,
    coarse_node_second,
):
    core = lax.rem(lax.axis_index("dom"), 2)
    members = membership.reshape(ROWS // 128, 128)
    my_links = coarse_links.T
    their_links = sibling(my_links)
    held, edge_held, near, far = halo_rows(features, send_rows, edge_first)
    near, far = sibling(near), across(far)
    projected, self_part, early, node_part = local_parts(held, neighbors.T, edge_held, node_first)
    near, far, their_links = lax.optimization_barrier((near, far, their_links))
    updated, first = fine_stage(
        held, projected, self_part, early, node_part, near, far, neighbors.T, members,
        edge_held, edge_second, node_first, node_second,
    )
    links = jnp.where(
        core == 0,
        jnp.concatenate([my_links, their_links], axis=1),
        jnp.concatenate([their_links, my_links], axis=1),
    )
    mine = (kept(updated, members, first).astype(F32) + sibling(first).astype(F32)).astype(BF16)
    two = across(jnp.concatenate([mine[:CHIP], mine[2 * CHIP :]], axis=0), 2)
    one = across(mine, 1)
    prepared = link_rows(links, coarse_edge_first, coarse_edge_second, coarse_node_first, coarse_node_second)
    one, two, prepared = lax.optimization_barrier((one, two, prepared))
    own_rows, far_rows, near_rows = prepared[:3]
    weights = prepared[3:]
    passed = totals(mine, one, two)
    got = sibling(passed)
    early = far_parts(passed, far_rows, weights[0])
    coarse_new = coarse_stage(mine, passed, got, early, own_rows, near_rows, *weights)
    far = across(coarse_new)
    partial, far_rows, near_rows = spread(updated, coarse_new, members)
    far, partial = lax.optimization_barrier((far, partial))
    near = sibling(far)
    return unpooled(partial, far_rows, near_rows, far, near)


def solution(mesh):
    placed = (
        P(("grp", "dom"), None),
        P(("grp", "dom"), None),
        P(("grp", "dom"), None),
        P(("grp", "dom")),
        P(("grp", "dom"), None),
        P(),
        P(),
        P(),
        P(),
        P(),
        P(),
        P(),
        P(),
    )
    return jax.shard_map(
        shards, mesh=mesh, in_specs=placed, out_specs=P(("grp", "dom"), None), check_vma=False
    )
```

```python
import jax
import jax.numpy as jnp
from jax import lax
from jax.experimental import pallas as pl
from jax.experimental.pallas import tpu as pltpu
from jax.sharding import PartitionSpec as P

H = 512
ROWS = 1024
HALO = 128
OWNED = 64
CHIP = 128
TILE = 512
PACK = 2 * CHIP + 16
DOM = 32
F32 = jnp.float32
BF16 = jnp.bfloat16

SIBLING = [(i, i ^ 1) for i in range(DOM)]


def facing(parts, step):
    pairs = []
    for part in range(parts):
        other = part ^ 1 if (part ^ 1) < parts else part
        for i in range(DOM):
            j = i + 2 * step - 1 if i % 2 else i - 2 * step + 1
            pairs.append((part * DOM + i, part * DOM + j if 0 <= j < DOM else other * DOM + i))
    return pairs


def sibling(value):
    return lax.ppermute(value, "dom", SIBLING)


def across(value, step=1):
    return lax.ppermute(value, ("grp", "dom"), facing(lax.axis_size("grp"), step))


def place():
    device = lax.axis_index("dom")
    core = lax.rem(device, 2)
    chip = lax.div(device, 2)
    return core, chip, chip - 1 + 2 * core, chip + 1 - 2 * core


def dot(a, b):
    return jnp.dot(a, b, preferred_element_type=F32)


def gated(half):
    return half + half * jnp.tanh(half)


def columns(ids, span):
    spread = jnp.transpose(jnp.broadcast_to(ids, (128, 128))).astype(jnp.int16)
    lane = lax.broadcasted_iota(jnp.int32, (128, 128), 1).astype(jnp.int16)
    one, zero = jnp.ones((), BF16), jnp.zeros((), BF16)
    return jnp.concatenate(
        [jnp.where(spread == lane + jnp.int16(128 * j), one, zero) for j in range(span // 128)], axis=1
    )


def layer_norm(values):
    average = jnp.mean(values, axis=-1, keepdims=True)
    centred = values - average
    variance = jnp.mean(centred * centred, axis=-1, keepdims=True)
    return centred * lax.rsqrt(variance + 1e-05)


def node_update(rows, node_part, total, through, node_second):
    hidden = gated(node_part + dot(total.astype(BF16), through)).astype(BF16)
    return (rows.astype(F32) + layer_norm(dot(hidden, node_second))).astype(BF16)


def product(edge_second, node_other):
    return (0.5 * dot(edge_second, node_other)).astype(BF16)


def pieces(source, target, arrived, count):
    step = source.shape[0] // count
    return [
        pltpu.make_async_copy(source.at[pl.ds(j * step, step), :], target.at[pl.ds(j * step, step), :], arrived.at[j])
        for j in range(count)
    ]


def halo_body(features, send_rows, edge_first, held, edge_other, near, far, ids, ids_arrived, arrived, edge_arrived):
    core = lax.rem(lax.axis_index("dom"), 2)
    ids_copy = pltpu.make_async_copy(send_rows, ids, ids_arrived)
    ids_copy.start()
    copies = pieces(features, held, arrived, 4)
    edge_copies = pieces(edge_first.at[pl.ds(H, H), :], edge_other, edge_arrived, 2)
    for copy in copies + edge_copies:
        copy.start()
    ids_copy.wait()
    up, down = ids[0:1, :], ids[1:2, :]
    chosen = jnp.concatenate(
        [columns(jnp.where(core == 0, up, down), ROWS), columns(jnp.where(core == 0, down, up), ROWS)], axis=0
    )
    for copy in copies:
        copy.wait()
    rows = dot(chosen, held[...]).astype(BF16)
    near[...] = rows[:HALO, :]
    far[...] = rows[HALO:, :]
    for copy in edge_copies:
        copy.wait()


def local_body(
    features, neighbors, edge_other, edge_first, node_first, edge_second, node_second,
    projected, self_part, early, node_part, through, last, ids, edge_self, node_held, second, arrived, first_arrived,
):
    ids_copy = pltpu.make_async_copy(neighbors, ids, first_arrived.at[0])
    edge_copy = pltpu.make_async_copy(edge_first.at[pl.ds(0, H), :], edge_self, first_arrived.at[1])
    copies = [
        pltpu.make_async_copy(node_first, node_held, arrived.at[0]),
        pltpu.make_async_copy(edge_second, second, arrived.at[1]),
        pltpu.make_async_copy(node_second, last, arrived.at[2]),
    ]
    for copy in [ids_copy, edge_copy] + copies:
        copy.start()
    projected[...] = (0.5 * dot(features[...], edge_other[...])).astype(BF16)
    ids_copy.wait()
    chosen = jnp.concatenate([columns(ids[0:1, s : s + 128], ROWS) for s in range(0, ROWS, 128)], axis=0)
    early[...] = dot(chosen, projected[...])
    edge_copy.wait()
    self_part[...] = 0.5 * dot(features[...], edge_self[...])
    for copy in copies:
        copy.wait()
    node_part[...] = 0.5 * dot(features[...], node_held[:H, :])
    through[...] = product(second[...], node_held[H:, :])


def pool(chips, membership, updated):
    row = lax.broadcasted_iota(jnp.int32, (CHIP, 128), 0)
    target = jnp.concatenate([chip * CHIP + row for chip in chips], axis=0)
    belongs = jnp.concatenate(
        [
            jnp.where(membership[j : j + 1, :] == target, jnp.ones((), F32), jnp.zeros((), F32)).astype(BF16)
            for j in range(ROWS // 128)
        ],
        axis=1,
    )
    count = lax.dot_general(
        jnp.ones((16, ROWS), BF16), belongs, (((1,), (1,)), ((), ())), preferred_element_type=F32
    )
    high = jnp.floor(count * (1.0 / 64.0))
    digit = lax.broadcasted_iota(jnp.int32, count.shape, 0)
    return dot(belongs, updated).astype(BF16), jnp.where(digit == 0, high, count - 64.0 * high).astype(BF16)


def divided(sums, count):
    whole = jnp.maximum(64.0 * count[0:1, :] + count[1:2, :], 1.0)
    column = jnp.transpose(jnp.broadcast_to(whole, (CHIP, 128)))
    return (sums / jnp.concatenate([column] * (H // 128), axis=1)).astype(BF16)


def fine_body(
    features, local, self_part, early, node_part, near, far, neighbors, membership, edge_other, through, last,
    updated, first, projected,
):
    device = lax.axis_index("dom")
    core = lax.rem(device, 2)
    projected[0:ROWS, :] = local[...]
    below = jnp.where(core == 0, far[...], near[...])
    above = jnp.where(core == 0, near[...], far[...])
    halo = jnp.concatenate([below, above], axis=0)
    projected[ROWS:, :] = (0.5 * dot(halo, edge_other[...])).astype(BF16)

    for tile in range(ROWS // TILE):
        here = slice(tile * TILE, (tile + 1) * TILE)
        spans = range(tile * TILE, (tile + 1) * TILE, 128)
        chosen = jnp.concatenate(
            [columns(neighbors[0:1, s : s + 128] - ROWS, 2 * HALO) for s in spans], axis=0
        )
        total = gated(self_part[here, :] + early[here, :] + dot(chosen, projected[ROWS:, :]))
        for k in range(1, 4):
            chosen = jnp.concatenate(
                [columns(neighbors[k : k + 1, s : s + 128], ROWS + 2 * HALO) for s in spans], axis=0
            )
            total = total + gated(self_part[here, :] + dot(chosen, projected[...]))
        updated[here, :] = node_update(features[here, :], node_part[here, :], total, through[...], last[...])

    _, chip, _, near_chip = place()
    first[: 2 * CHIP, :], counts = pool((near_chip, chip), membership, updated[...])
    first[2 * CHIP :, :] = jnp.concatenate([counts, jnp.zeros((16, H - 2 * CHIP), BF16)], axis=1)


def keep_body(updated, membership, first, keep):
    _, _, far_chip, _ = place()
    keep[:CHIP, :], counts = pool((far_chip,), membership, updated[...])
    keep[CHIP:, :] = first[CHIP:, :]
    keep[2 * CHIP :, :CHIP] = counts


def totals_body(mine, one, two, passed):
    core, chip, _, _ = place()
    reach = jnp.where(core == 0, chip, DOM // 2 - 1 - chip)
    has_one = jnp.where(reach >= 1, 1.0, 0.0)
    has_two = jnp.where(reach >= 2, 1.0, 0.0)
    counts = slice(2 * CHIP, PACK)
    sums = mine[:CHIP, :].astype(F32) + has_one * one[CHIP : 2 * CHIP, :].astype(F32)
    sums = sums + has_two * two[:CHIP, :].astype(F32)
    count = mine[counts, :CHIP].astype(F32) + has_one * one[counts, CHIP : 2 * CHIP].astype(F32)
    count = count + has_two * two[CHIP:, :CHIP].astype(F32)
    passed[:CHIP, :] = divided(sums, count)
    passed[CHIP : 2 * CHIP, :] = (has_one * one[:CHIP, :].astype(F32)).astype(BF16)
    passed[counts, :] = (has_one * one[counts, :].astype(F32)).astype(BF16)


def links_body(
    links, edge_first, edge_second, node_first, node_second,
    own_rows, far_rows, near_rows, edge_first_held, node_first_held, node_second_held, through, second, arrived,
):
    copies = [
        pltpu.make_async_copy(source, target, arrived.at[i])
        for i, (source, target) in enumerate(
            (
                (edge_first, edge_first_held),
                (edge_second, second),
                (node_first, node_first_held),
                (node_second, node_second_held),
            )
        )
    ]
    for copy in copies:
        copy.start()
    _, chip, far_chip, near_chip = place()
    for rows, which in ((own_rows, chip), (far_rows, far_chip), (near_rows, near_chip)):
        for k in range(8):
            rows[k * CHIP : (k + 1) * CHIP, :] = columns(links[k : k + 1, :] - which * CHIP, CHIP)
    for copy in copies:
        copy.wait()
    through[...] = product(second[...], node_first_held[H:, :])


def far_body(passed, far_rows, edge_first, other):
    projected = (0.5 * dot(passed[:CHIP, :], edge_first[H:, :])).astype(BF16)
    other[...] = dot(far_rows[...], projected)


def coarse_body(
    mine, passed, got, early, own_rows, near_rows, edge_first, node_first, node_second, through, updated
):
    counts = slice(2 * CHIP, PACK)
    between = passed[CHIP : 2 * CHIP, :].astype(F32) + got[CHIP : 2 * CHIP, :].astype(F32)
    count = passed[counts, :CHIP].astype(F32) + got[counts, :CHIP].astype(F32)
    coarse = divided(
        mine[CHIP : 2 * CHIP, :].astype(F32) + between, mine[counts, CHIP : 2 * CHIP].astype(F32) + count
    )
    self_part = 0.5 * dot(coarse, edge_first[:H, :])
    node_part = 0.5 * dot(coarse, node_first[:H, :])
    both = jnp.concatenate([coarse, got[:CHIP, :]], axis=0)
    projected = (0.5 * dot(both, edge_first[H:, :])).astype(BF16)
    other = early[...] + dot(jnp.concatenate([own_rows[...], near_rows[...]], axis=1), projected)
    total = jnp.zeros((CHIP, H), F32)
    for k in range(8):
        total = total + gated(self_part + other[k * CHIP : (k + 1) * CHIP, :])
    updated[...] = node_update(coarse, node_part, total, through[...], node_second[...])


def spread_body(fine, coarse, membership, partial, far_rows, near_rows):
    device = lax.axis_index("dom")
    core = lax.rem(device, 2)
    chip = lax.div(device, 2)
    for j in range(ROWS // 256):
        here = slice(j * 256, (j + 1) * 256)

        def rows_of(which):
            return jnp.concatenate(
                [columns(membership[2 * j + i : 2 * j + i + 1, :] - which * CHIP, CHIP) for i in range(2)], axis=0
            )

        partial[here, :] = fine[here, :].astype(F32) + dot(rows_of(chip), coarse[...])
        far_rows[here, :] = rows_of(chip - 1 + 2 * core)
        near_rows[here, :] = rows_of(chip + 1 - 2 * core)


def unpool_body(partial, far_rows, near_rows, far, near, result, made, sent):
    lookup = jnp.concatenate([far[...], near[...]], axis=0)
    copies = []
    for j in range(ROWS // 256):
        here = slice(j * 256, (j + 1) * 256)
        chosen = jnp.concatenate([far_rows[here, :], near_rows[here, :]], axis=1)
        made[here, :] = (partial[here, :] + dot(chosen, lookup)).astype(BF16)
        copy = pltpu.make_async_copy(
            made.at[pl.ds(j * 256, 256), :], result.at[pl.ds(j * 256, 256), :], sent.at[j]
        )
        copy.start()
        copies.append(copy)
    for copy in copies:
        copy.wait()


VMEM = pl.BlockSpec(memory_space=pltpu.VMEM)
ANY = pl.BlockSpec(memory_space=pltpu.HBM)


def call(body, outs, scratch, flops, args, apart=(), out_spec=VMEM):
    args = [pltpu.with_memory_space_constraint(a, pltpu.HBM) if i in apart else a for i, a in enumerate(args)]
    return pl.pallas_call(
        body,
        out_shape=[jax.ShapeDtypeStruct(shape, kind) for shape, kind in outs],
        in_specs=[ANY if i in apart else VMEM for i in range(len(args))],
        out_specs=[out_spec] * len(outs),
        scratch_shapes=scratch,
        compiler_params=pltpu.CompilerParams(vmem_limit_bytes=24 * 1024 * 1024),
        cost_estimate=pl.CostEstimate(flops=flops, bytes_accessed=4 * 1024 * 1024, transcendentals=0),
    )(*args)


def halo_rows(*args):
    return call(
        halo_body,
        [((ROWS, H), BF16), ((H, H), BF16), ((HALO, H), BF16), ((HALO, H), BF16)],
        [
            pltpu.VMEM((2, HALO), jnp.int32),
            pltpu.SemaphoreType.DMA(()),
            pltpu.SemaphoreType.DMA((4,)),
            pltpu.SemaphoreType.DMA((2,)),
        ],
        300000000,
        args,
        (0, 1, 2),
    )


def local_parts(*args):
    return call(
        local_body,
        [((ROWS, H), BF16)] + [((ROWS, H), F32)] * 3 + [((H, H), BF16)] * 2 + [((4, ROWS), jnp.int32)],
        [
            pltpu.VMEM((H, H), BF16),
            pltpu.VMEM((2 * H, H), BF16),
            pltpu.VMEM((H, H), BF16),
            pltpu.SemaphoreType.DMA((3,)),
            pltpu.SemaphoreType.DMA((2,)),
        ],
        2600000000,
        args,
        (1, 3, 4, 5, 6),
    )


def fine_stage(*args):
    return call(
        fine_body,
        [((ROWS, H), BF16), ((PACK, H), BF16)],
        [pltpu.VMEM((ROWS + 2 * HALO, H), BF16)],
        7000000000,
        args,
    )


def kept(*args):
    return call(keep_body, [((PACK, H), BF16)], [], 200000000, args)[0]


def totals(*args):
    return call(totals_body, [((PACK, H), BF16)], [], 100000000, args)[0]


def link_rows(*args):
    return call(
        links_body,
        [((8 * CHIP, CHIP), BF16)] * 3 + [((2 * H, H), BF16)] * 2 + [((H, H), BF16)] * 2,
        [pltpu.VMEM((H, H), BF16), pltpu.SemaphoreType.DMA((4,))],
        400000000,
        args,
        (1, 2, 3, 4),
    )


def far_parts(*args):
    return call(far_body, [((8 * CHIP, H), F32)], [], 200000000, args)[0]


def coarse_stage(*args):
    return call(coarse_body, [((CHIP, H), BF16)], [], 1000000000, args)[0]


def spread(*args):
    return call(spread_body, [((ROWS, H), F32), ((ROWS, CHIP), BF16), ((ROWS, CHIP), BF16)], [], 400000000, args)


def unpooled(*args):
    return call(
        unpool_body,
        [((ROWS, H), BF16)],
        [pltpu.VMEM((ROWS, H), BF16), pltpu.SemaphoreType.DMA((4,))],
        400000000,
        args,
        (),
        ANY,
    )[0]


def shards(
    features,
    send_rows,
    neighbors,
    membership,
    coarse_links,
    edge_first,
    edge_second,
    node_first,
    node_second,
    coarse_edge_first,
    coarse_edge_second,
    coarse_node_first,
    coarse_node_second,
):
    core = lax.rem(lax.axis_index("dom"), 2)
    members = membership.reshape(ROWS // 128, 128)
    my_links = coarse_links.T
    their_links = sibling(my_links)
    held, edge_other, near, far = halo_rows(features, send_rows, edge_first)
    near, far = sibling(near), across(far)
    projected, self_part, early, node_part, through, last, ids = local_parts(
        held, neighbors.T, edge_other, edge_first, node_first, edge_second, node_second
    )
    near, far, their_links = lax.optimization_barrier((near, far, their_links))
    updated, first = fine_stage(
        held, projected, self_part, early, node_part, near, far, ids, members, edge_other, through, last
    )
    links = jnp.where(
        core == 0,
        jnp.concatenate([my_links, their_links], axis=1),
        jnp.concatenate([their_links, my_links], axis=1),
    )
    mine = (kept(updated, members, first).astype(F32) + sibling(first).astype(F32)).astype(BF16)
    two = across(jnp.concatenate([mine[:CHIP], mine[2 * CHIP :]], axis=0), 2)
    one = across(mine, 1)
    prepared = link_rows(links, coarse_edge_first, coarse_edge_second, coarse_node_first, coarse_node_second)
    one, two, prepared = lax.optimization_barrier((one, two, prepared))
    own_rows, far_rows, near_rows = prepared[:3]
    weights = prepared[3:]
    passed = totals(mine, one, two)
    got = sibling(passed)
    early = far_parts(passed, far_rows, weights[0])
    coarse_new = coarse_stage(mine, passed, got, early, own_rows, near_rows, *weights)
    far = across(coarse_new)
    partial, far_rows, near_rows = spread(updated, coarse_new, members)
    far, partial = lax.optimization_barrier((far, partial))
    near = sibling(far)
    return unpooled(partial, far_rows, near_rows, far, near)


def solution(mesh):
    placed = (
        P(("grp", "dom"), None),
        P(("grp", "dom"), None),
        P(("grp", "dom"), None),
        P(("grp", "dom")),
        P(("grp", "dom"), None),
        P(),
        P(),
        P(),
        P(),
        P(),
        P(),
        P(),
        P(),
    )
    return jax.shard_map(
        shards, mesh=mesh, in_specs=placed, out_specs=P(("grp", "dom"), None), check_vma=False
    )
```

```python
import jax
import jax.numpy as jnp
from jax import lax
from jax.experimental import pallas as pl
from jax.experimental.pallas import tpu as pltpu
from jax.sharding import PartitionSpec as P

H = 512
ROWS = 1024
HALO = 128
OWNED = 64
CHIP = 128
TILE = 512
PACK = 2 * CHIP + 16
DOM = 32
F32 = jnp.float32
BF16 = jnp.bfloat16

SIBLING = [(i, i ^ 1) for i in range(DOM)]


def facing(parts, step):
    pairs = []
    for part in range(parts):
        other = part ^ 1 if (part ^ 1) < parts else part
        for i in range(DOM):
            j = i + 2 * step - 1 if i % 2 else i - 2 * step + 1
            pairs.append((part * DOM + i, part * DOM + j if 0 <= j < DOM else other * DOM + i))
    return pairs


def sibling(value):
    return lax.ppermute(value, "dom", SIBLING)


def across(value, step=1):
    return lax.ppermute(value, ("grp", "dom"), facing(lax.axis_size("grp"), step))


def place():
    device = lax.axis_index("dom")
    core = lax.rem(device, 2)
    chip = lax.div(device, 2)
    return core, chip, chip - 1 + 2 * core, chip + 1 - 2 * core


def dot(a, b):
    return jnp.dot(a, b, preferred_element_type=F32)


def gated(half):
    return half + half * jnp.tanh(half)


def columns(ids, span):
    spread = jnp.transpose(jnp.broadcast_to(ids, (128, 128))).astype(jnp.int16)
    lane = lax.broadcasted_iota(jnp.int32, (128, 128), 1).astype(jnp.int16)
    one, zero = jnp.ones((), BF16), jnp.zeros((), BF16)
    return jnp.concatenate(
        [jnp.where(spread == lane + jnp.int16(128 * j), one, zero) for j in range(span // 128)], axis=1
    )


def layer_norm(values):
    average = jnp.mean(values, axis=-1, keepdims=True)
    centred = values - average
    variance = jnp.mean(centred * centred, axis=-1, keepdims=True)
    return centred * lax.rsqrt(variance + 1e-05)


def node_update(rows, node_part, total, through, node_second):
    hidden = gated(node_part + dot(total.astype(BF16), through)).astype(BF16)
    return (rows.astype(F32) + layer_norm(dot(hidden, node_second))).astype(BF16)


def product(edge_second, node_other):
    return (0.5 * dot(edge_second, node_other)).astype(BF16)


def pieces(source, target, arrived, count):
    step = source.shape[0] // count
    return [
        pltpu.make_async_copy(source.at[pl.ds(j * step, step), :], target.at[pl.ds(j * step, step), :], arrived.at[j])
        for j in range(count)
    ]


def halo_body(
    features, send_rows, edge_first, neighbors, held, edge_other, sources, near, far,
    ids, ids_arrived, arrived, edge_arrived, sources_arrived,
):
    core = lax.rem(lax.axis_index("dom"), 2)
    ids_copy = pltpu.make_async_copy(send_rows, ids, ids_arrived)
    ids_copy.start()
    copies = pieces(features, held, arrived, 4)
    edge_copies = pieces(edge_first.at[pl.ds(H, H), :], edge_other, edge_arrived, 2)
    edge_copies.append(pltpu.make_async_copy(neighbors, sources, sources_arrived))
    for copy in copies + edge_copies:
        copy.start()
    ids_copy.wait()
    up, down = ids[0:1, :], ids[1:2, :]
    chosen = jnp.concatenate(
        [columns(jnp.where(core == 0, up, down), ROWS), columns(jnp.where(core == 0, down, up), ROWS)], axis=0
    )
    for copy in copies:
        copy.wait()
    rows = dot(chosen, held[...]).astype(BF16)
    near[...] = rows[:HALO, :]
    far[...] = rows[HALO:, :]
    for copy in edge_copies:
        copy.wait()


def local_body(
    features, neighbors, edge_other, edge_first, node_first, edge_second,
    projected, self_part, early, node_part, through, edge_self, node_held, second, arrived, first_arrived,
):
    edge_copy = pltpu.make_async_copy(edge_first.at[pl.ds(0, H), :], edge_self, first_arrived)
    copies = [
        pltpu.make_async_copy(node_first, node_held, arrived.at[0]),
        pltpu.make_async_copy(edge_second, second, arrived.at[1]),
    ]
    for copy in [edge_copy] + copies:
        copy.start()
    projected[...] = (0.5 * dot(features[...], edge_other[...])).astype(BF16)
    chosen = jnp.concatenate([columns(neighbors[0:1, s : s + 128], ROWS) for s in range(0, ROWS, 128)], axis=0)
    early[...] = dot(chosen, projected[...])
    edge_copy.wait()
    self_part[...] = 0.5 * dot(features[...], edge_self[...])
    for copy in copies:
        copy.wait()
    node_part[...] = 0.5 * dot(features[...], node_held[:H, :])
    through[...] = product(second[...], node_held[H:, :])


def pool(chips, membership, updated):
    row = lax.broadcasted_iota(jnp.int32, (CHIP, 128), 0)
    target = jnp.concatenate([chip * CHIP + row for chip in chips], axis=0)
    belongs = jnp.concatenate(
        [
            jnp.where(membership[j : j + 1, :] == target, jnp.ones((), F32), jnp.zeros((), F32)).astype(BF16)
            for j in range(ROWS // 128)
        ],
        axis=1,
    )
    count = lax.dot_general(
        jnp.ones((16, ROWS), BF16), belongs, (((1,), (1,)), ((), ())), preferred_element_type=F32
    )
    high = jnp.floor(count * (1.0 / 64.0))
    digit = lax.broadcasted_iota(jnp.int32, count.shape, 0)
    return dot(belongs, updated).astype(BF16), jnp.where(digit == 0, high, count - 64.0 * high).astype(BF16)


def divided(sums, count):
    whole = jnp.maximum(64.0 * count[0:1, :] + count[1:2, :], 1.0)
    column = jnp.transpose(jnp.broadcast_to(whole, (CHIP, 128)))
    return (sums / jnp.concatenate([column] * (H // 128), axis=1)).astype(BF16)


def fine_body(
    features, local, self_part, early, node_part, near, far, neighbors, membership, edge_other, through, node_second,
    updated, first, projected,
):
    device = lax.axis_index("dom")
    core = lax.rem(device, 2)
    projected[0:ROWS, :] = local[...]
    below = jnp.where(core == 0, far[...], near[...])
    above = jnp.where(core == 0, near[...], far[...])
    halo = jnp.concatenate([below, above], axis=0)
    projected[ROWS:, :] = (0.5 * dot(halo, edge_other[...])).astype(BF16)

    for tile in range(ROWS // TILE):
        here = slice(tile * TILE, (tile + 1) * TILE)
        spans = range(tile * TILE, (tile + 1) * TILE, 128)
        chosen = jnp.concatenate(
            [columns(neighbors[0:1, s : s + 128] - ROWS, 2 * HALO) for s in spans], axis=0
        )
        total = gated(self_part[here, :] + early[here, :] + dot(chosen, projected[ROWS:, :]))
        for k in range(1, 4):
            chosen = jnp.concatenate(
                [columns(neighbors[k : k + 1, s : s + 128], ROWS + 2 * HALO) for s in spans], axis=0
            )
            total = total + gated(self_part[here, :] + dot(chosen, projected[...]))
        updated[here, :] = node_update(features[here, :], node_part[here, :], total, through[...], node_second[...])

    _, chip, _, near_chip = place()
    first[: 2 * CHIP, :], counts = pool((near_chip, chip), membership, updated[...])
    first[2 * CHIP :, :] = jnp.concatenate([counts, jnp.zeros((16, H - 2 * CHIP), BF16)], axis=1)


def keep_body(updated, membership, first, keep):
    _, _, far_chip, _ = place()
    keep[:CHIP, :], counts = pool((far_chip,), membership, updated[...])
    keep[CHIP:, :] = first[CHIP:, :]
    keep[2 * CHIP :, :CHIP] = counts


def totals_body(mine, one, two, passed):
    core, chip, _, _ = place()
    reach = jnp.where(core == 0, chip, DOM // 2 - 1 - chip)
    has_one = jnp.where(reach >= 1, 1.0, 0.0)
    has_two = jnp.where(reach >= 2, 1.0, 0.0)
    counts = slice(2 * CHIP, PACK)
    sums = mine[:CHIP, :].astype(F32) + has_one * one[CHIP : 2 * CHIP, :].astype(F32)
    sums = sums + has_two * two[:CHIP, :].astype(F32)
    count = mine[counts, :CHIP].astype(F32) + has_one * one[counts, CHIP : 2 * CHIP].astype(F32)
    count = count + has_two * two[CHIP:, :CHIP].astype(F32)
    passed[:CHIP, :] = divided(sums, count)
    passed[CHIP : 2 * CHIP, :] = (has_one * one[:CHIP, :].astype(F32)).astype(BF16)
    passed[counts, :] = (has_one * one[counts, :].astype(F32)).astype(BF16)


def links_body(
    links, edge_first, edge_second, node_first, node_second,
    own_rows, far_rows, near_rows, edge_first_held, node_first_held, node_second_held, through, second, arrived,
):
    copies = [
        pltpu.make_async_copy(source, target, arrived.at[i])
        for i, (source, target) in enumerate(
            (
                (edge_first, edge_first_held),
                (edge_second, second),
                (node_first, node_first_held),
                (node_second, node_second_held),
            )
        )
    ]
    for copy in copies:
        copy.start()
    _, chip, far_chip, near_chip = place()
    for rows, which in ((own_rows, chip), (far_rows, far_chip), (near_rows, near_chip)):
        for k in range(8):
            rows[k * CHIP : (k + 1) * CHIP, :] = columns(links[k : k + 1, :] - which * CHIP, CHIP)
    for copy in copies:
        copy.wait()
    through[...] = product(second[...], node_first_held[H:, :])


def far_body(passed, far_rows, edge_first, other):
    projected = (0.5 * dot(passed[:CHIP, :], edge_first[H:, :])).astype(BF16)
    other[...] = dot(far_rows[...], projected)


def coarse_body(
    mine, passed, got, early, own_rows, near_rows, edge_first, node_first, node_second, through, updated
):
    counts = slice(2 * CHIP, PACK)
    between = passed[CHIP : 2 * CHIP, :].astype(F32) + got[CHIP : 2 * CHIP, :].astype(F32)
    count = passed[counts, :CHIP].astype(F32) + got[counts, :CHIP].astype(F32)
    coarse = divided(
        mine[CHIP : 2 * CHIP, :].astype(F32) + between, mine[counts, CHIP : 2 * CHIP].astype(F32) + count
    )
    self_part = 0.5 * dot(coarse, edge_first[:H, :])
    node_part = 0.5 * dot(coarse, node_first[:H, :])
    both = jnp.concatenate([coarse, got[:CHIP, :]], axis=0)
    projected = (0.5 * dot(both, edge_first[H:, :])).astype(BF16)
    other = early[...] + dot(jnp.concatenate([own_rows[...], near_rows[...]], axis=1), projected)
    total = jnp.zeros((CHIP, H), F32)
    for k in range(8):
        total = total + gated(self_part + other[k * CHIP : (k + 1) * CHIP, :])
    updated[...] = node_update(coarse, node_part, total, through[...], node_second[...])


def spread_body(fine, coarse, membership, partial, far_rows, near_rows):
    device = lax.axis_index("dom")
    core = lax.rem(device, 2)
    chip = lax.div(device, 2)
    for j in range(ROWS // 256):
        here = slice(j * 256, (j + 1) * 256)

        def rows_of(which):
            return jnp.concatenate(
                [columns(membership[2 * j + i : 2 * j + i + 1, :] - which * CHIP, CHIP) for i in range(2)], axis=0
            )

        partial[here, :] = fine[here, :].astype(F32) + dot(rows_of(chip), coarse[...])
        far_rows[here, :] = rows_of(chip - 1 + 2 * core)
        near_rows[here, :] = rows_of(chip + 1 - 2 * core)


def reach_body(partial, far_rows, far, grown):
    for j in range(ROWS // 256):
        here = slice(j * 256, (j + 1) * 256)
        grown[here, :] = partial[here, :] + dot(far_rows[here, :], far[...])


def unpool_body(partial, near_rows, near, result, made, sent):
    copies = []
    for j in range(ROWS // 256):
        here = slice(j * 256, (j + 1) * 256)
        made[here, :] = (partial[here, :] + dot(near_rows[here, :], near[...])).astype(BF16)
        copy = pltpu.make_async_copy(
            made.at[pl.ds(j * 256, 256), :], result.at[pl.ds(j * 256, 256), :], sent.at[j]
        )
        copy.start()
        copies.append(copy)
    for copy in copies:
        copy.wait()


VMEM = pl.BlockSpec(memory_space=pltpu.VMEM)
ANY = pl.BlockSpec(memory_space=pltpu.HBM)


def call(body, outs, scratch, flops, args, apart=(), out_spec=VMEM):
    args = [pltpu.with_memory_space_constraint(a, pltpu.HBM) if i in apart else a for i, a in enumerate(args)]
    return pl.pallas_call(
        body,
        out_shape=[jax.ShapeDtypeStruct(shape, kind) for shape, kind in outs],
        in_specs=[ANY if i in apart else VMEM for i in range(len(args))],
        out_specs=[out_spec] * len(outs),
        scratch_shapes=scratch,
        compiler_params=pltpu.CompilerParams(vmem_limit_bytes=24 * 1024 * 1024),
        cost_estimate=pl.CostEstimate(flops=flops, bytes_accessed=4 * 1024 * 1024, transcendentals=0),
    )(*args)


def halo_rows(*args):
    return call(
        halo_body,
        [((ROWS, H), BF16), ((H, H), BF16), ((4, ROWS), jnp.int32), ((HALO, H), BF16), ((HALO, H), BF16)],
        [
            pltpu.VMEM((2, HALO), jnp.int32),
            pltpu.SemaphoreType.DMA(()),
            pltpu.SemaphoreType.DMA((4,)),
            pltpu.SemaphoreType.DMA((2,)),
            pltpu.SemaphoreType.DMA(()),
        ],
        300000000,
        args,
        (0, 1, 2, 3),
    )


def local_parts(*args):
    return call(
        local_body,
        [((ROWS, H), BF16)] + [((ROWS, H), F32)] * 3 + [((H, H), BF16)],
        [
            pltpu.VMEM((H, H), BF16),
            pltpu.VMEM((2 * H, H), BF16),
            pltpu.VMEM((H, H), BF16),
            pltpu.SemaphoreType.DMA((2,)),
            pltpu.SemaphoreType.DMA(()),
        ],
        2600000000,
        args,
        (3, 4, 5),
    )


def fine_stage(*args):
    return call(
        fine_body,
        [((ROWS, H), BF16), ((PACK, H), BF16)],
        [pltpu.VMEM((ROWS + 2 * HALO, H), BF16)],
        7000000000,
        args,
    )


def kept(*args):
    return call(keep_body, [((PACK, H), BF16)], [], 200000000, args)[0]


def totals(*args):
    return call(totals_body, [((PACK, H), BF16)], [], 100000000, args)[0]


def link_rows(*args):
    return call(
        links_body,
        [((8 * CHIP, CHIP), BF16)] * 3 + [((2 * H, H), BF16)] * 2 + [((H, H), BF16)] * 2,
        [pltpu.VMEM((H, H), BF16), pltpu.SemaphoreType.DMA((4,))],
        400000000,
        args,
        (1, 2, 3, 4),
    )


def far_parts(*args):
    return call(far_body, [((8 * CHIP, H), F32)], [], 200000000, args)[0]


def coarse_stage(*args):
    return call(coarse_body, [((CHIP, H), BF16)], [], 1000000000, args)[0]


def spread(*args):
    return call(spread_body, [((ROWS, H), F32), ((ROWS, CHIP), BF16), ((ROWS, CHIP), BF16)], [], 400000000, args)


def reached(*args):
    return call(reach_body, [((ROWS, H), F32)], [], 200000000, args)[0]


def unpooled(*args):
    return call(
        unpool_body,
        [((ROWS, H), BF16)],
        [pltpu.VMEM((ROWS, H), BF16), pltpu.SemaphoreType.DMA((4,))],
        400000000,
        args,
        (),
        ANY,
    )[0]


def shards(
    features,
    send_rows,
    neighbors,
    membership,
    coarse_links,
    edge_first,
    edge_second,
    node_first,
    node_second,
    coarse_edge_first,
    coarse_edge_second,
    coarse_node_first,
    coarse_node_second,
):
    core = lax.rem(lax.axis_index("dom"), 2)
    members = membership.reshape(ROWS // 128, 128)
    my_links = coarse_links.T
    their_links = sibling(my_links)
    held, edge_other, sources, near, far = halo_rows(features, send_rows, edge_first, neighbors.T)
    near, far = sibling(near), across(far)
    projected, self_part, early, node_part, through = local_parts(
        held, sources, edge_other, edge_first, node_first, edge_second
    )
    near, far, their_links = lax.optimization_barrier((near, far, their_links))
    updated, first = fine_stage(
        held, projected, self_part, early, node_part, near, far, sources, members, edge_other, through, node_second
    )
    links = jnp.where(
        core == 0,
        jnp.concatenate([my_links, their_links], axis=1),
        jnp.concatenate([their_links, my_links], axis=1),
    )
    mine = (kept(updated, members, first).astype(F32) + sibling(first).astype(F32)).astype(BF16)
    two = across(jnp.concatenate([mine[:CHIP], mine[2 * CHIP :]], axis=0), 2)
    one = across(mine, 1)
    prepared = link_rows(links, coarse_edge_first, coarse_edge_second, coarse_node_first, coarse_node_second)
    one, two, prepared = lax.optimization_barrier((one, two, prepared))
    own_rows, far_rows, near_rows = prepared[:3]
    weights = prepared[3:]
    passed = totals(mine, one, two)
    got = sibling(passed)
    early = far_parts(passed, far_rows, weights[0])
    coarse_new = coarse_stage(mine, passed, got, early, own_rows, near_rows, *weights)
    far = across(coarse_new)
    partial, far_rows, near_rows = spread(updated, coarse_new, members)
    far, partial = lax.optimization_barrier((far, partial))
    near = sibling(far)
    return unpooled(reached(partial, far_rows, far), near_rows, near)


def solution(mesh):
    placed = (
        P(("grp", "dom"), None),
        P(("grp", "dom"), None),
        P(("grp", "dom"), None),
        P(("grp", "dom")),
        P(("grp", "dom"), None),
        P(),
        P(),
        P(),
        P(),
        P(),
        P(),
        P(),
        P(),
    )
    return jax.shard_map(
        shards, mesh=mesh, in_specs=placed, out_specs=P(("grp", "dom"), None), check_vma=False
    )
```
